512 devices in a mesh: run: 32 (over y_lo, x, core), tp: 16 (over z, y_hi).
Axes of the slice: x: 4, y: 8 (y_hi: 2, y_lo: 4; y = y_hi * 4 + y_lo), z: 8, core: 2. Of those that a mesh axis runs over, the one named last changes fastest.
Arguments:
- tokens: bfloat16 [16384, 4096], P('run', 'tp'), may hold values from -6 to 6
- output_gradient: bfloat16 [16384, 4096], P('run', 'tp'), may hold values from -6 to 6
- frozen_weight: bfloat16 [4096, 4096], P('tp'), may hold values from -0.09375 to 0.09375
- adapter_down: bfloat16 [32, 4096, 128], P('run', 'tp'), may hold values from -4 to 4
- adapter_up: bfloat16 [32, 128, 4096], P('run', None, 'tp'), may hold values from -4 to 4
- down_adam_moments: float32 [32, 2, 4096, 128], P('run', None, 'tp'), as said below
- up_adam_moments: float32 [32, 2, 128, 4096], P('run', None, None, 'tp'), as said below
- feature_factors: float32 [32, 2, 4096], P('run', None, 'tp'), may hold values from 0.003 to 0.3
- rank_factors: float32 [32, 2, 128], P('run'), may hold values from 0.003 to 0.3
- run_adapter_ranks: int32 [16], replicated, may hold values from 16 to 128, as said below
- run_optimizers: int32 [16], replicated, may hold values from 0 to 1, as said below
- run_owner_slots: int32 [16], replicated, may hold values from 0 to 31, as said below
Outputs:
- layer_output: bfloat16 [16384, 4096], P('run', 'tp')
- input_gradient: bfloat16 [16384, 4096], P('run', 'tp')
- new_down: bfloat16 [32, 4096, 128], P('run', 'tp')
- new_up: bfloat16 [32, 128, 4096], P('run', None, 'tp')
- new_adam_down: float32 [32, 2, 4096, 128], P('run', None, 'tp')
- new_adam_up: float32 [32, 2, 128, 4096], P('run', None, None, 'tp')
- new_factor_wide: float32 [32, 2, 4096], P('run', None, 'tp')
- new_factor_rank: float32 [32, 2, 128], P('run')
The draws below stay inside these ranges and needn't reach their ends.
Inputs may be any that keep to these rules, and one draw needn't show every extreme that they name: `run_adapter_ranks`: some run has rank 128 and some run has rank 16. `run_optimizers`: 0 is Adam, 1 is Adafactor; both occur. `run_owner_slots`: distinct slots; slots 0 and 32 - 1 are always owned; half of the slots are owned by no run. `down_adam_moments`: index 0 holds first moments within -4 to 4, index 1 positive second moments. `up_adam_moments`: index 0 holds first moments within -4 to 4, index 1 positive second moments.
All inputs are finite; a program needn't handle non-finite values.
Results may differ from the reference program's by a relative error of at most 0.02.
Values may be sent and summed in bfloat16 or wider, within the bound.
No kernel may reach another device: no remote copies, remote signals or barrier semaphores. Data moves between devices by JAX's collectives and lax.ppermute only.
A program may use at most 64 MiB of HBM per device.

```python
import math
import jax
import jax.numpy as jnp
from jax import lax

MODEL_WIDTH = 4096
ADAPTER_RANK_TOP = 128
RANK_MIN = 16
RUN_COUNT = 16
RUN_ROWS = 32
TOKEN_TOTAL = 16384
N_RUN = 32
N_TP = 16


def positive_field(key, array_shape, lower_end, upper_end):
    return jnp.exp(jax.random.uniform(key, array_shape, jnp.float32, jnp.log(lower_end), jnp.log(upper_end)))


def draw_down_adam_moments(key, part):
    key = jax.random.fold_in(key, 31)
    first_key, second_key = jax.random.split(key)
    array_shape = (N_RUN, MODEL_WIDTH, ADAPTER_RANK_TOP)
    first_part = jnp.clip(jax.random.normal(first_key, array_shape, jnp.float32), -4.0, 4.0)
    second_part = positive_field(second_key, array_shape, 0.01, 0.3)
    return jnp.stack([first_part, second_part], axis=1)


def draw_up_adam_moments(key, part):
    key = jax.random.fold_in(key, 37)
    first_key, second_key = jax.random.split(key)
    array_shape = (N_RUN, ADAPTER_RANK_TOP, MODEL_WIDTH)
    first_part = jnp.clip(jax.random.normal(first_key, array_shape, jnp.float32), -4.0, 4.0)
    second_part = positive_field(second_key, array_shape, 0.01, 0.3)
    return jnp.stack([first_part, second_part], axis=1)


def draw_run_adapter_ranks(key, part):
    key = jax.random.fold_in(key, 41)
    value_key, shuffle_key = jax.random.split(key)
    values = jax.random.randint(value_key, (RUN_COUNT,), RANK_MIN, ADAPTER_RANK_TOP + 1)
    shuffle = jax.random.permutation(shuffle_key, RUN_COUNT)
    values = values.at[shuffle[0]].set(ADAPTER_RANK_TOP)
    values = values.at[shuffle[1]].set(RANK_MIN)
    return values.astype(jnp.int32)


def draw_run_optimizers(key, part):
    key = jax.random.fold_in(key, 43)
    value_key, shuffle_key = jax.random.split(key)
    values = jax.random.randint(value_key, (RUN_COUNT,), 0, 2)
    shuffle = jax.random.permutation(shuffle_key, RUN_COUNT)
    values = values.at[shuffle[0]].set(0)
    values = values.at[shuffle[1]].set(1)
    return values.astype(jnp.int32)


def draw_run_owner_slots(key, part):
    key = jax.random.fold_in(key, 47)
    middle_key, shuffle_key = jax.random.split(key)
    middle = 1 + jax.random.permutation(middle_key, N_RUN - 2)[:RUN_COUNT - 2]
    chosen = jnp.concatenate([jnp.array([0, N_RUN - 1], jnp.int32), middle.astype(jnp.int32)])
    shuffle = jax.random.permutation(shuffle_key, RUN_COUNT)
    return chosen[shuffle].astype(jnp.int32)


def block_levels(own_key, dims, cuts, least, high):
    loudness, own = 1.0, jax.random.fold_in(own_key, 6)
    for dim, blocks in cuts:
        draws = jnp.exp(jax.random.uniform(jax.random.fold_in(own, dim), (blocks,), jnp.float32, least / len(cuts), high / len(cuts)))
        loudness = loudness * jnp.repeat(draws, dims[dim] // blocks).reshape([-1 if axis == dim else 1 for axis in range(len(dims))])
    return loudness


def noise(rng, dims, deviation, most, pieces=(), kind=jnp.bfloat16):
    values = jax.random.normal(rng, dims, jnp.float32) * deviation
    if len(pieces) > 0:
        values = block_levels(rng, dims, pieces, -0.22, 0.18) * values
    return jnp.clip(values, min=-most, max=most).astype(kind)


def setup_inputs(seed: int = 0) -> dict:
    splits = jax.random.split(jax.random.key(seed), 13)
    tokens = noise(splits[0], (TOKEN_TOTAL, MODEL_WIDTH), 1.0, 6.0, ((0, 32), (1, 16)))
    output_gradient = noise(splits[1], (TOKEN_TOTAL, MODEL_WIDTH), 1.0, 6.0, ((0, 32), (1, 16)))
    frozen_weight = noise(splits[2], (MODEL_WIDTH, MODEL_WIDTH), MODEL_WIDTH ** -0.5, 0.09375, ((0, 16),))
    adapter_down = noise(splits[3], (N_RUN, MODEL_WIDTH, ADAPTER_RANK_TOP), 1.0, 4.0, ((0, 32), (1, 16)))
    adapter_up = noise(splits[4], (N_RUN, ADAPTER_RANK_TOP, MODEL_WIDTH), 1.0, 4.0, ((0, 32), (2, 16)))
    down_adam_moments = draw_down_adam_moments(jax.random.fold_in(splits[12], 71), 0)
    up_adam_moments = draw_up_adam_moments(jax.random.fold_in(splits[12], 71), 0)
    feature_factors = jnp.clip(jnp.exp(math.log(0.3) - 4.6051702 * jax.random.uniform(splits[7], (N_RUN, 2, MODEL_WIDTH), jnp.float32) ** block_levels(splits[7], (N_RUN, 2, MODEL_WIDTH), ((0, 32), (2, 16)), -0.2, 0.2)), 0.003, 0.3)
    rank_factors = jnp.clip(jnp.exp(math.log(0.3) - 4.6051702 * jax.random.uniform(splits[8], (N_RUN, 2, ADAPTER_RANK_TOP), jnp.float32) ** block_levels(splits[8], (N_RUN, 2, ADAPTER_RANK_TOP), ((0, 32),), -0.2, 0.2)), 0.003, 0.3)
    run_adapter_ranks = draw_run_adapter_ranks(jax.random.fold_in(splits[12], 71), 0)
    run_optimizers = draw_run_optimizers(jax.random.fold_in(splits[12], 71), 0)
    run_owner_slots = draw_run_owner_slots(jax.random.fold_in(splits[12], 71), 0)
    return dict(tokens=tokens, output_gradient=output_gradient, frozen_weight=frozen_weight, adapter_down=adapter_down, adapter_up=adapter_up, down_adam_moments=down_adam_moments, up_adam_moments=up_adam_moments, feature_factors=feature_factors, rank_factors=rank_factors, run_adapter_ranks=run_adapter_ranks, run_optimizers=run_optimizers, run_owner_slots=run_owner_slots)


beta_first = 0.9
beta_second = 0.99
adam_rate = 0.05
adam_eps = 1e-08
factor_rate = 0.05
factor_decay = 0.99
adapter_alpha = 0.5

def base_blocks(tokens, frozen_weight):
    feature_width = MODEL_WIDTH // N_TP
    token_blocks = tokens.reshape(TOKEN_TOTAL, N_TP, feature_width).transpose(1, 0, 2)
    weight_blocks = frozen_weight.reshape(N_TP, feature_width, MODEL_WIDTH)

    def add_block(running, block_pair):
        rounded = jnp.dot(block_pair[0], block_pair[1], preferred_element_type=jnp.float32).astype(jnp.bfloat16)
        rounded = lax.optimization_barrier(rounded)
        return (running + rounded.astype(jnp.float32), None)
    summed, ignored = lax.scan(add_block, jnp.zeros((TOKEN_TOTAL, MODEL_WIDTH), jnp.float32), (token_blocks, weight_blocks))
    return summed

def adam_step(weights, first_moment, second_moment, gradient, keep_mask):
    first_new = beta_first * first_moment + (1.0 - beta_first) * gradient
    second_new = beta_second * second_moment + (1.0 - beta_second) * gradient * gradient
    updated = weights.astype(jnp.float32) - adam_rate * first_new / (jnp.sqrt(second_new) + adam_eps)
    return (updated * keep_mask, first_new * keep_mask, second_new * keep_mask)

def reference(tokens, output_gradient, frozen_weight, adapter_down, adapter_up, down_adam_moments, up_adam_moments, feature_factors, rank_factors, run_adapter_ranks, run_optimizers, run_owner_slots):
    frozen_total = base_blocks(tokens, frozen_weight)
    backward_total = jnp.dot(output_gradient, frozen_weight.T, preferred_element_type=jnp.float32)
    inverse_root = 1.0 / math.sqrt(MODEL_WIDTH)
    selected_down = adapter_down[run_owner_slots].astype(jnp.float32)
    selected_up = adapter_up[run_owner_slots].astype(jnp.float32)
    rank_as_float = run_adapter_ranks.astype(jnp.float32)
    run_scaling = adapter_alpha / jnp.sqrt(rank_as_float)
    keep_mask = (jnp.arange(ADAPTER_RANK_TOP, dtype=jnp.int32)[None, :] < run_adapter_ranks[:, None]).astype(jnp.float32)
    token_runs = tokens.reshape(N_RUN, RUN_COUNT, RUN_ROWS, MODEL_WIDTH).astype(jnp.float32)
    grad_runs = output_gradient.reshape(N_RUN, RUN_COUNT, RUN_ROWS, MODEL_WIDTH).astype(jnp.float32)
    row_mask = keep_mask[None, :, None, :]
    low_rows = (jnp.einsum('nrkd,rdq->nrkq', token_runs, selected_down) * inverse_root * row_mask).astype(jnp.bfloat16)
    back_rows = (jnp.einsum('nrkd,rqd->nrkq', grad_runs, selected_up) * row_mask).astype(jnp.bfloat16)
    lowrank_wide = low_rows.astype(jnp.float32)
    backward_wide = back_rows.astype(jnp.float32)
    adapter_output = run_scaling[None, :, None, None] * jnp.einsum('chov,hvy->choy', lowrank_wide, selected_up)
    adapter_backward = (run_scaling * inverse_root)[None, :, None, None] * jnp.einsum('ibfv,bav->ibfa', backward_wide, selected_down)
    layer_output = (frozen_total + adapter_output.reshape(TOKEN_TOTAL, MODEL_WIDTH)).astype(jnp.bfloat16)
    input_gradient = (backward_total + adapter_backward.reshape(TOKEN_TOTAL, MODEL_WIDTH)).astype(jnp.bfloat16)
    grad_up = run_scaling[:, None, None] * jnp.einsum('nrkq,nrkd->rqd', lowrank_wide, grad_runs)
    grad_down = (run_scaling * inverse_root)[:, None, None] * jnp.einsum('nrkd,nrkq->rdq', token_runs, backward_wide)
    keep_down = keep_mask[:, None, :]
    keep_up = keep_mask[:, :, None]
    slot_adam_down = down_adam_moments[run_owner_slots]
    slot_adam_up = up_adam_moments[run_owner_slots]
    adam_new_down, first_down, second_down = adam_step(selected_down, slot_adam_down[:, 0], slot_adam_down[:, 1], grad_down, keep_down)
    adam_new_up, first_up, second_up = adam_step(selected_up, slot_adam_up[:, 0], slot_adam_up[:, 1], grad_up, keep_up)
    slot_wide = feature_factors[run_owner_slots]
    slot_rank = rank_factors[run_owner_slots]
    square_down = grad_down * grad_down
    row_new_down = factor_decay * slot_wide[:, 0] + (1.0 - factor_decay) * lax.optimization_barrier(jnp.sum(square_down, axis=2)) / rank_as_float[:, None]
    col_new_down = (factor_decay * slot_rank[:, 0] + (1.0 - factor_decay) * lax.optimization_barrier(jnp.sum(square_down, axis=1)) / MODEL_WIDTH) * keep_mask
    mean_down = lax.optimization_barrier(jnp.sum(row_new_down, axis=1)) / MODEL_WIDTH
    col_safe = jnp.where(keep_mask > 0, col_new_down, 1.0)
    step_down = grad_down * jnp.sqrt(mean_down[:, None, None] / (row_new_down[:, :, None] * col_safe[:, None, :]))
    fact_down = (selected_down - factor_rate * step_down) * keep_down
    square_up = grad_up * grad_up
    row_new_up = (factor_decay * slot_rank[:, 1] + (1.0 - factor_decay) * lax.optimization_barrier(jnp.sum(square_up, axis=2)) / MODEL_WIDTH) * keep_mask
    col_new_up = factor_decay * slot_wide[:, 1] + (1.0 - factor_decay) * lax.optimization_barrier(jnp.sum(square_up, axis=1)) / rank_as_float[:, None]
    mean_up = lax.optimization_barrier(jnp.sum(row_new_up, axis=1)) / rank_as_float
    row_safe = jnp.where(keep_mask > 0, row_new_up, 1.0)
    step_up = grad_up * jnp.sqrt(mean_up[:, None, None] / (row_safe[:, :, None] * col_new_up[:, None, :]))
    fact_up = (selected_up - factor_rate * step_up) * keep_up
    is_adam = run_optimizers == 0
    flag_three = is_adam[:, None, None]
    flag_four = is_adam[:, None, None, None]
    run_down = jnp.where(flag_three, adam_new_down, fact_down).astype(jnp.bfloat16)
    run_up = jnp.where(flag_three, adam_new_up, fact_up).astype(jnp.bfloat16)
    run_adam_down = jnp.where(flag_four, jnp.stack([first_down, second_down], axis=1), slot_adam_down)
    run_adam_up = jnp.where(flag_four, jnp.stack([first_up, second_up], axis=1), slot_adam_up)
    run_wide = jnp.where(flag_three, slot_wide, jnp.stack([row_new_down, col_new_up], axis=1))
    run_rank = jnp.where(flag_three, slot_rank, jnp.stack([col_new_down, row_new_up], axis=1))
    new_down = jnp.zeros((N_RUN, MODEL_WIDTH, ADAPTER_RANK_TOP), jnp.bfloat16).at[run_owner_slots].set(run_down)
    new_up = jnp.zeros((N_RUN, ADAPTER_RANK_TOP, MODEL_WIDTH), jnp.bfloat16).at[run_owner_slots].set(run_up)
    new_adam_down = jnp.zeros((N_RUN, 2, MODEL_WIDTH, ADAPTER_RANK_TOP), jnp.float32).at[run_owner_slots].set(run_adam_down)
    new_adam_up = jnp.zeros((N_RUN, 2, ADAPTER_RANK_TOP, MODEL_WIDTH), jnp.float32).at[run_owner_slots].set(run_adam_up)
    new_factor_wide = jnp.zeros((N_RUN, 2, MODEL_WIDTH), jnp.float32).at[run_owner_slots].set(run_wide)
    new_factor_rank = jnp.zeros((N_RUN, 2, ADAPTER_RANK_TOP), jnp.float32).at[run_owner_slots].set(run_rank)
    return (layer_output, input_gradient, new_down, new_up, new_adam_down, new_adam_up, new_factor_wide, new_factor_rank)
```

```python
import functools
import math

import jax
import jax.numpy as jnp
from jax import lax
from jax.experimental import pallas as pl
from jax.experimental.pallas import tpu as pltpu
from jax.sharding import PartitionSpec as P

RANK_MIN = 16

beta_first = 0.9
beta_second = 0.99
adam_rate = 0.05
adam_eps = 1e-08
factor_rate = 0.05
factor_decay = 0.99
adapter_alpha = 0.5

F32 = jnp.float32
BF16 = jnp.bfloat16
SMEM = pl.BlockSpec(memory_space=pltpu.SMEM)
PARAMS = pltpu.CompilerParams(vmem_limit_bytes=60 * 1024 * 1024)


def shape(dims, dtype):
    return jax.ShapeDtypeStruct(dims, dtype)


def whole(dims, index=None):
    if index is None:
        return pl.BlockSpec(dims, lambda step: (0,) * len(dims))
    return pl.BlockSpec((None,) + dims[1:], lambda step: (index,) + (0,) * (len(dims) - 1))


def staged_call(body, out_shape, scalars, operands, after=()):
    used, extra = len(scalars) + len(operands), len(after)
    pairs = [operand if isinstance(operand, tuple) else (operand, None) for operand in operands]

    def without_extra(*refs):
        body(*refs[:used], *refs[used + extra :])

    return pl.pallas_call(
        without_extra,
        out_shape=out_shape,
        grid=(1,),
        in_specs=[SMEM] * len(scalars)
        + [whole(operand.shape, index) for operand, index in pairs]
        + [pl.BlockSpec(memory_space=pl.ANY)] * extra,
        out_specs=tuple(whole(out.shape) for out in out_shape),
        compiler_params=PARAMS,
    )(*scalars, *[operand for operand, _ in pairs], *after)


def contract(left_side, right_side, left_dim, right_dim):
    return lax.dot_general(
        left_side,
        right_side,
        (((left_dim,), (right_dim,)), ((), ())),
        preferred_element_type=F32,
    )


def all_to_all(blocks, axis):
    return lax.all_to_all(blocks, axis, split_axis=0, concat_axis=0, tiled=True)


def to_column(row):
    extent = row.shape[1]
    eye = lax.broadcasted_iota(jnp.int32, (extent, extent), 0) == lax.broadcasted_iota(
        jnp.int32, (extent, extent), 1
    )
    return jnp.sum(jnp.where(eye, row, 0.0), axis=1, keepdims=True)


def to_row(column):
    extent = column.shape[0]
    eye = lax.broadcasted_iota(jnp.int32, (extent, extent), 0) == lax.broadcasted_iota(
        jnp.int32, (extent, extent), 1
    )
    return jnp.sum(jnp.where(eye, column, 0.0), axis=0, keepdims=True)


def own_run(place_ref, slots_ref, ranks_ref, kinds_ref):
    rank, kind, holds = jnp.int32(RANK_MIN), jnp.int32(0), jnp.int32(0)
    for run in range(slots_ref.shape[0]):
        owned = slots_ref[run] == place_ref[0]
        rank = jnp.where(owned, ranks_ref[run], rank)
        kind = jnp.where(owned, kinds_ref[run], kind)
        holds = jnp.where(owned, 1, holds)
    return rank, kind, holds


def scatter_kernel(slots_ref, tok_ref, grad_ref, out_ref):
    run_count = slots_ref.shape[0]
    rows = tok_ref.shape[0] // run_count
    out_ref[...] = jnp.zeros_like(out_ref)
    for run in range(run_count):
        slot = slots_ref[run]
        out_ref[slot, :rows, :] = tok_ref[run * rows : (run + 1) * rows, :]
        out_ref[slot, rows:, :] = grad_ref[run * rows : (run + 1) * rows, :]


def partial_kernel(place_ref, tok_ref, weight_ref, after_ref, out_ref):
    width = out_ref.shape[3]
    product = jnp.dot(tok_ref[...], weight_ref[...], preferred_element_type=F32)
    for part in range(out_ref.shape[1]):
        out_ref[0, part] = product[:, part * width : (part + 1) * width].astype(out_ref.dtype)


def backward_kernel(place_ref, own_ref, other_ref, weight_ref, out_ref):
    width = out_ref.shape[1]
    half = place_ref[1]
    first = pl.ds(pl.multiple_of(half * width, width), width)
    second = pl.ds(pl.multiple_of((1 - half) * width, width), width)

    @pl.when(pl.program_id(0) == 0)
    def _():
        out_ref[...] = jnp.zeros_like(out_ref)

    out_ref[...] += contract(own_ref[0], weight_ref[:, first], 1, 1) + contract(
        other_ref[0], weight_ref[:, second], 1, 1
    )


def low_kernel(recv_ref, down_ref, up_ref, out_ref):
    slots, both_rows, width = recv_ref.shape
    rows = both_rows // 2
    rank = down_ref.shape[2]
    tok = recv_ref[:, :rows, :].reshape(slots * rows, width)
    grad = recv_ref[:, rows:, :].reshape(slots * rows, width)
    low = contract(tok, down_ref[0], 1, 0).astype(out_ref.dtype)
    back = contract(grad, up_ref[0], 1, 1).astype(out_ref.dtype)
    blocks, block_rows, _ = out_ref.shape
    out_ref[:, :, :rank] = low.reshape(blocks, block_rows, rank)
    out_ref[:, :, rank:] = back.reshape(blocks, block_rows, rank)


def reduce_kernel(inverse_root, place_ref, slots_ref, ranks_ref, kinds_ref, part_ref, out_ref):
    rank, _, _ = own_run(place_ref, slots_ref, ranks_ref, kinds_ref)
    extent = part_ref.shape[2] // 2
    column = lax.broadcasted_iota(jnp.int32, (1, 2 * extent), 1)
    keep = (jnp.where(column < extent, column, column - extent) < rank).astype(F32)
    factor = keep * jnp.where(column < extent, F32(inverse_root), F32(1.0))
    total = part_ref[0].astype(F32)
    for block in range(1, part_ref.shape[0]):
        total += part_ref[block].astype(F32)
    rounded = (total * factor).astype(out_ref.dtype)
    for block in range(out_ref.shape[0]):
        out_ref[block] = rounded


def scale_row(rank, extent):
    return adapter_alpha / jnp.sqrt(jnp.full((1, extent), rank, jnp.int32).astype(F32))


def home_kernel(
    inverse_root, place_ref, slots_ref, ranks_ref, kinds_ref, low_ref, down_ref, up_ref, out_ref
):
    rank, _, _ = own_run(place_ref, slots_ref, ranks_ref, kinds_ref)
    slots, both_rows, width = out_ref.shape
    rows = both_rows // 2
    extent = down_ref.shape[2]
    scale = scale_row(rank, width)
    low = low_ref[:, :, :extent].reshape(slots * rows, extent)
    back = low_ref[:, :, extent:].reshape(slots * rows, extent)
    forward = scale * contract(low, up_ref[0], 1, 0)
    backward = (scale * inverse_root) * contract(back, down_ref[0], 1, 1)
    out_ref[:, :rows, :] = forward.astype(out_ref.dtype).reshape(slots, rows, width)
    out_ref[:, rows:, :] = backward.astype(out_ref.dtype).reshape(slots, rows, width)


def grad_kernel(
    inverse_root,
    place_ref,
    slots_ref,
    ranks_ref,
    kinds_ref,
    recv_ref,
    low_ref,
    wide_ref,
    down_ref,
    up_ref,
    wide_new_ref,
    sums_ref,
):
    rank, _, _ = own_run(place_ref, slots_ref, ranks_ref, kinds_ref)
    slots, both_rows, width = recv_ref.shape
    rows = both_rows // 2
    extent = low_ref.shape[2] // 2
    tok = recv_ref[:, :rows, :].reshape(slots * rows, width)
    grad = recv_ref[:, rows:, :].reshape(slots * rows, width)
    low = low_ref[:, :, :extent].reshape(slots * rows, extent)
    back = low_ref[:, :, extent:].reshape(slots * rows, extent)
    grad_up = scale_row(rank, width) * contract(low, grad, 0, 0)
    grad_down = (scale_row(rank, extent) * inverse_root) * contract(tok, back, 0, 0)
    up_ref[...] = grad_up
    down_ref[...] = grad_down
    square_up = grad_up * grad_up
    square_down = grad_down * grad_down
    rank_row = jnp.full((1, width), rank, jnp.int32).astype(F32)
    row_new = (
        factor_decay * wide_ref[0, 0:1, :]
        + (1.0 - factor_decay) * to_row(jnp.sum(square_down, axis=1, keepdims=True)) / rank_row
    )
    col_new = (
        factor_decay * wide_ref[0, 1:2, :]
        + (1.0 - factor_decay) * jnp.sum(square_up, axis=0, keepdims=True) / rank_row
    )
    wide_new_ref[0, 0:1, :] = row_new
    wide_new_ref[0, 1:2, :] = col_new
    col_part = jnp.sum(square_down, axis=0, keepdims=True)
    row_part = to_row(jnp.sum(square_up, axis=1, keepdims=True))
    total = jnp.broadcast_to(jnp.sum(row_new, axis=1, keepdims=True), (1, extent))
    sums = jnp.concatenate(
        [col_part, row_part, total, jnp.zeros((sums_ref.shape[0] - 3, extent), F32)], axis=0
    )
    sums_ref[...] = sums


def update_kernel(
    full_width,
    place_ref,
    slots_ref,
    ranks_ref,
    kinds_ref,
    grad_down_ref,
    grad_up_ref,
    wide_new_ref,
    sums_ref,
    down_ref,
    up_ref,
    down_moments_ref,
    up_moments_ref,
    wide_ref,
    rank_ref,
    new_down_ref,
    new_up_ref,
    new_down_moments_ref,
    new_up_moments_ref,
    new_wide_ref,
    new_rank_ref,
):
    rank, kind, holds = own_run(place_ref, slots_ref, ranks_ref, kinds_ref)
    extent = sums_ref.shape[1]
    is_adam = kind == 0
    held = holds == 1
    keep_row = (lax.broadcasted_iota(jnp.int32, (1, extent), 1) < rank).astype(F32)
    keep_column = (lax.broadcasted_iota(jnp.int32, (extent, 1), 0) < rank).astype(F32)
    rank_row = jnp.full((1, extent), rank, jnp.int32).astype(F32)
    sums = sums_ref[...]
    col_new = (
        factor_decay * rank_ref[0, 0:1, :] + (1.0 - factor_decay) * sums[0:1, :] / full_width
    ) * keep_row
    row_new = (
        factor_decay * rank_ref[0, 1:2, :] + (1.0 - factor_decay) * sums[1:2, :] / full_width
    ) * keep_row
    mean_down = sums[2:3, :] / full_width
    mean_up = jnp.sum(row_new, axis=1, keepdims=True) / rank_row
    col_safe = jnp.where(keep_row > 0, col_new, 1.0)
    row_safe = to_column(jnp.where(keep_row > 0, row_new, 1.0))
    wide_row = wide_new_ref[0, 0:1, :]
    wide_col = wide_new_ref[0, 1:2, :]

    def adam(weights, moments_ref, gradient):
        first = beta_first * moments_ref[0, 0] + (1.0 - beta_first) * gradient
        second = beta_second * moments_ref[0, 1] + (1.0 - beta_second) * gradient * gradient
        return weights - adam_rate * first / (jnp.sqrt(second) + adam_eps), first, second

    def finish(weights_ref, moments_ref, gradient, step, keep, new_ref, new_moments_ref):
        weights = weights_ref[0].astype(F32)
        updated, first, second = adam(weights, moments_ref, gradient)
        factored = weights - factor_rate * step
        value = jnp.where(is_adam, updated, factored) * keep
        new_ref[0] = jnp.where(held, value, 0.0).astype(new_ref.dtype)
        new_moments_ref[0, 0] = jnp.where(
            held, jnp.where(is_adam, first * keep, moments_ref[0, 0]), 0.0
        )
        new_moments_ref[0, 1] = jnp.where(
            held, jnp.where(is_adam, second * keep, moments_ref[0, 1]), 0.0
        )

    grad_down = grad_down_ref[...]
    step_down = grad_down * jnp.sqrt(mean_down / (to_column(wide_row) * col_safe))
    finish(
        down_ref,
        down_moments_ref,
        grad_down,
        step_down,
        keep_row,
        new_down_ref,
        new_down_moments_ref,
    )
    grad_up = grad_up_ref[...]
    step_up = grad_up * jnp.sqrt(mean_up[:, :1] / (row_safe * wide_col))
    finish(
        up_ref, up_moments_ref, grad_up, step_up, keep_column, new_up_ref, new_up_moments_ref
    )
    new_wide_ref[0] = jnp.where(held, jnp.where(is_adam, wide_ref[0], wide_new_ref[0]), 0.0)
    new_rank_ref[0, 0:1, :] = jnp.where(
        held, jnp.where(is_adam, rank_ref[0, 0:1, :], col_new), 0.0
    )
    new_rank_ref[0, 1:2, :] = jnp.where(
        held, jnp.where(is_adam, rank_ref[0, 1:2, :], row_new), 0.0
    )


def output_kernel(slots_ref, own_ref, other_ref, backward_ref, home_ref, layer_ref, input_ref):
    both_rows = home_ref.shape[1]
    rows = both_rows // 2
    for run in range(slots_ref.shape[0]):
        here = slice(run * rows, (run + 1) * rows)
        terms = home_ref[slots_ref[run]].astype(F32)
        layer_ref[here, :] = (
            own_ref[here, :] + other_ref[here, :].astype(F32) + terms[:rows]
        ).astype(layer_ref.dtype)
        input_ref[here, :] = (backward_ref[here, :] + terms[rows:]).astype(input_ref.dtype)


def ring_kernel(*refs):
    count = len(refs) // 3
    for index in range(count):
        message_ref, block_ref, out_ref = refs[2 * index], refs[2 * index + 1], refs[2 * count + index]
        out_ref[...] = (message_ref[...].astype(F32) + block_ref[...].astype(F32)).astype(
            out_ref.dtype
        )


def first_kernel(*refs):
    low_kernel(*refs[:3], refs[7])
    ring_kernel(*refs[3:7], *refs[8:])


def second_kernel(inverse_root, *refs):
    reduce_kernel(inverse_root, *refs[:5], refs[9])
    ring_kernel(*refs[5:9], *refs[10:])


def third_kernel(inverse_root, *refs):
    home_kernel(inverse_root, *refs[:7], refs[9])
    ring_kernel(*refs[7:9], refs[10])


def add_kernel(left_ref, right_ref, out_ref):
    out_ref[...] = left_ref[...] + right_ref[...]


def sum_kernel(place_ref, up_ref, down_ref, block_ref, own_ref, send_ref):
    half = place_ref[1]

    def total(index):
        return (
            up_ref[index].astype(F32)
            + down_ref[index].astype(F32)
            + block_ref[index].astype(F32)
        )

    own_ref[...] = total(half)
    send_ref[...] = total(1 - half).astype(send_ref.dtype)


def local(
    tokens,
    output_gradient,
    frozen_weight,
    adapter_down,
    adapter_up,
    down_adam_moments,
    up_adam_moments,
    feature_factors,
    rank_factors,
    run_adapter_ranks,
    run_optimizers,
    run_owner_slots,
):
    slot_count = lax.axis_size("run")
    tp_count = lax.axis_size("tp")
    ring_length = tp_count // 2
    token_rows, width = tokens.shape
    full_width = frozen_weight.shape[1]
    rank_extent = adapter_down.shape[2]
    run_count = run_adapter_ranks.shape[0]
    run_rows = token_rows // run_count
    inverse_root = 1.0 / math.sqrt(full_width)
    position = lax.axis_index("run")
    tp_self = lax.axis_index("tp")
    half_self = lax.rem(tp_self, 2)
    z_self = tp_self // 2
    place = jnp.stack(
        [position, half_self]
        + [lax.rem(z_self + offset, ring_length) for offset in range(ring_length)]
    ).astype(jnp.int32)
    run_facts = (place, run_owner_slots, run_adapter_ranks, run_optimizers)
    swap_pairs = [(index, index ^ 1) for index in range(tp_count)]
    up_pairs = [(index, (index + 2) % tp_count) for index in range(tp_count)]
    down_pairs = [(index, (index - 2) % tp_count) for index in range(tp_count)]
    z_groups = [[z * 2 + half for z in range(ring_length)] for half in range(2)]

    (to_owner,) = staged_call(
        scatter_kernel,
        (shape((slot_count, 2 * run_rows, width), BF16),),
        (run_owner_slots,),
        (tokens, output_gradient),
    )
    recv = all_to_all(to_owner, "run")

    def from_every_z(values):
        return lax.all_gather(
            values[None], "tp", axis=0, tiled=True, axis_index_groups=z_groups
        )

    grad_own = from_every_z(output_gradient)
    swapped = lax.ppermute(output_gradient, "tp", swap_pairs)
    grad_other = from_every_z(swapped)

    partial = pl.pallas_call(
        partial_kernel,
        out_shape=shape((ring_length, 2, token_rows, width), BF16),
        grid_spec=pltpu.PrefetchScalarGridSpec(
            num_scalar_prefetch=1,
            grid=(ring_length,),
            in_specs=[
                pl.BlockSpec((token_rows, width), lambda i, place: (0, 0)),
                pl.BlockSpec((width, 2 * width), lambda i, place: (0, place[2 + i])),
                pl.BlockSpec(memory_space=pl.ANY),
            ],
            out_specs=pl.BlockSpec((1, 2, token_rows, width), lambda i, place: (i, 0, 0, 0)),
        ),
        compiler_params=PARAMS,
    )(place, tokens, frozen_weight, to_owner)
    up_steps = ring_length // 2
    down_steps = ring_length - 1 - up_steps
    upward, downward = partial[up_steps], partial[ring_length - down_steps]


    def hop_up(values):
        return lax.ppermute(values, "tp", up_pairs)

    def hop_down(values):
        return lax.ppermute(values, "tp", down_pairs)

    message = shape(upward.shape, BF16)

    def ring_operands(step, upward, downward):
        operands = (hop_up(upward), (partial, up_steps - step))
        if step < down_steps:
            operands += (hop_down(downward), (partial, ring_length - down_steps + step))
        return operands

    low_part, upward, downward = staged_call(
        first_kernel,
        (
            shape((tp_count, slot_count * run_rows // tp_count, 2 * rank_extent), BF16),
            message,
            message,
        ),
        (),
        (recv, adapter_down, adapter_up) + ring_operands(1, upward, downward),
        after=(swapped,),
    )
    low_blocks = all_to_all(low_part, "tp")
    low_own, upward, downward = staged_call(
        functools.partial(second_kernel, inverse_root),
        (shape(low_blocks.shape, BF16), message, message),
        run_facts,
        (low_blocks,) + ring_operands(2, upward, downward),
    )
    low_all = all_to_all(low_own, "tp")

    to_home, upward = staged_call(
        functools.partial(third_kernel, inverse_root),
        (shape((slot_count, 2 * run_rows, width), BF16), message),
        run_facts,
        (low_all, adapter_down, adapter_up) + ring_operands(3, upward, downward),
    )
    home = all_to_all(to_home, "run")

    grad_down, grad_up, wide_new, sums = staged_call(
        functools.partial(grad_kernel, inverse_root),
        (
            shape((width, rank_extent), F32),
            shape((rank_extent, width), F32),
            shape((1, 2, width), F32),
            shape((8, rank_extent), F32),
        ),
        run_facts,
        (recv, low_all, feature_factors),
        after=(to_home,),
    )

    def sum_hop(values, hop, after=()):
        other = lax.ppermute(values, "tp", [(index, index ^ hop) for index in range(tp_count)])
        return staged_call(add_kernel, (shape(values.shape, F32),), (), (values, other), after)[0]

    sums = sum_hop(sums, 2)
    base_own, base_send = staged_call(
        sum_kernel,
        (shape((token_rows, width), F32), shape((token_rows, width), BF16)),
        (place,),
        (hop_up(upward), hop_down(downward), (partial, 0)),
        after=(sums,),
    )
    base_other = lax.ppermute(base_send, "tp", swap_pairs)
    sums = sum_hop(sums, 4, (base_send,))
    sums = sum_hop(sums, 8)

    backward_total = pl.pallas_call(
        backward_kernel,
        out_shape=shape((token_rows, width), F32),
        grid_spec=pltpu.PrefetchScalarGridSpec(
            num_scalar_prefetch=1,
            grid=(ring_length,),
            in_specs=[
                pl.BlockSpec((1, token_rows, width), lambda i, place: (i, 0, 0)),
                pl.BlockSpec((1, token_rows, width), lambda i, place: (i, 0, 0)),
                pl.BlockSpec((width, 2 * width), lambda i, place: (0, i)),
            ],
            out_specs=pl.BlockSpec((token_rows, width), lambda i, place: (0, 0)),
        ),
        compiler_params=PARAMS,
    )(place, grad_own, grad_other, frozen_weight)
    sums = sum_hop(sums, 1, (backward_total,))
    updated = staged_call(
        functools.partial(update_kernel, full_width),
        (
            shape(adapter_down.shape, BF16),
            shape(adapter_up.shape, BF16),
            shape(down_adam_moments.shape, F32),
            shape(up_adam_moments.shape, F32),
            shape(feature_factors.shape, F32),
            shape(rank_factors.shape, F32),
        ),
        run_facts,
        (
            grad_down,
            grad_up,
            wide_new,
            sums,
            adapter_down,
            adapter_up,
            down_adam_moments,
            up_adam_moments,
            feature_factors,
            rank_factors,
        ),
    )

    layer_output, input_gradient = staged_call(
        output_kernel,
        (shape((token_rows, width), BF16),) * 2,
        (run_owner_slots,),
        (base_own, base_other, backward_total, home),
        after=(updated[5],),
    )
    return (layer_output, input_gradient) + tuple(updated)


def solution(mesh):
    placed = (
        P("run", "tp"),
        P("run", "tp"),
        P("tp", None),
        P("run", "tp", None),
        P("run", None, "tp"),
        P("run", None, "tp", None),
        P("run", None, None, "tp"),
        P("run", None, "tp"),
        P("run", None, None),
        P(),
        P(),
        P(),
    )
    return jax.shard_map(
        local,
        mesh=mesh,
        in_specs=placed,
        out_specs=(
            P("run", "tp"),
            P("run", "tp"),
            P("run", "tp", None),
            P("run", None, "tp"),
            P("run", None, "tp", None),
            P("run", None, None, "tp"),
            P("run", None, "tp"),
            P("run", None, None),
        ),
        check_vma=False,
    )
```

```python
import functools
import math

import jax
import jax.numpy as jnp
from jax import lax
from jax.experimental import pallas as pl
from jax.experimental.pallas import tpu as pltpu
from jax.sharding import PartitionSpec as P

RANK_MIN = 16

beta_first = 0.9
beta_second = 0.99
adam_rate = 0.05
adam_eps = 1e-08
factor_rate = 0.05
factor_decay = 0.99
adapter_alpha = 0.5

F32 = jnp.float32
BF16 = jnp.bfloat16
SMEM = pl.BlockSpec(memory_space=pltpu.SMEM)
PARAMS = pltpu.CompilerParams(vmem_limit_bytes=60 * 1024 * 1024)


def shape(dims, dtype):
    return jax.ShapeDtypeStruct(dims, dtype)


def whole(dims, index=None):
    if index is None:
        return pl.BlockSpec(dims, lambda step: (0,) * len(dims))
    return pl.BlockSpec((None,) + dims[1:], lambda step: (index,) + (0,) * (len(dims) - 1))


def staged_call(body, out_shape, scalars, operands, after=()):
    used, extra = len(scalars) + len(operands), len(after)
    pairs = [operand if isinstance(operand, tuple) else (operand, None) for operand in operands]

    def without_extra(*refs):
        body(*refs[:used], *refs[used + extra :])

    return pl.pallas_call(
        without_extra,
        out_shape=out_shape,
        grid=(1,),
        in_specs=[SMEM] * len(scalars)
        + [whole(operand.shape, index) for operand, index in pairs]
        + [pl.BlockSpec(memory_space=pl.ANY)] * extra,
        out_specs=tuple(whole(out.shape) for out in out_shape),
        compiler_params=PARAMS,
    )(*scalars, *[operand for operand, _ in pairs], *after)


def contract(left_side, right_side, left_dim, right_dim):
    return lax.dot_general(
        left_side,
        right_side,
        (((left_dim,), (right_dim,)), ((), ())),
        preferred_element_type=F32,
    )


def all_to_all(blocks, axis):
    return lax.all_to_all(blocks, axis, split_axis=0, concat_axis=0, tiled=True)


def to_column(row):
    extent = row.shape[1]
    eye = lax.broadcasted_iota(jnp.int32, (extent, extent), 0) == lax.broadcasted_iota(
        jnp.int32, (extent, extent), 1
    )
    return jnp.sum(jnp.where(eye, row, 0.0), axis=1, keepdims=True)


def to_row(column):
    extent = column.shape[0]
    eye = lax.broadcasted_iota(jnp.int32, (extent, extent), 0) == lax.broadcasted_iota(
        jnp.int32, (extent, extent), 1
    )
    return jnp.sum(jnp.where(eye, column, 0.0), axis=0, keepdims=True)


def own_run(place_ref, slots_ref, ranks_ref, kinds_ref):
    rank, kind, holds = jnp.int32(RANK_MIN), jnp.int32(0), jnp.int32(0)
    for run in range(slots_ref.shape[0]):
        owned = slots_ref[run] == place_ref[0]
        rank = jnp.where(owned, ranks_ref[run], rank)
        kind = jnp.where(owned, kinds_ref[run], kind)
        holds = jnp.where(owned, 1, holds)
    return rank, kind, holds


def scatter_kernel(slots_ref, tok_ref, grad_ref, out_ref):
    run_count = slots_ref.shape[0]
    rows = tok_ref.shape[0] // run_count
    out_ref[...] = jnp.zeros_like(out_ref)
    for run in range(run_count):
        slot = slots_ref[run]
        out_ref[slot, :rows, :] = tok_ref[run * rows : (run + 1) * rows, :]
        out_ref[slot, rows:, :] = grad_ref[run * rows : (run + 1) * rows, :]


def partial_kernel(place_ref, tok_ref, weight_ref, after_ref, out_ref):
    width = out_ref.shape[3]
    product = jnp.dot(tok_ref[...], weight_ref[...], preferred_element_type=F32)
    for part in range(out_ref.shape[1]):
        out_ref[0, part] = product[:, part * width : (part + 1) * width].astype(out_ref.dtype)


def backward_kernel(place_ref, own_ref, other_ref, weight_ref, out_ref):
    width = out_ref.shape[1]
    half = place_ref[1]
    first = pl.ds(pl.multiple_of(half * width, width), width)
    second = pl.ds(pl.multiple_of((1 - half) * width, width), width)

    @pl.when(pl.program_id(0) == 0)
    def _():
        out_ref[...] = jnp.zeros_like(out_ref)

    out_ref[...] += contract(own_ref[0], weight_ref[:, first], 1, 1) + contract(
        other_ref[0], weight_ref[:, second], 1, 1
    )


def low_kernel(recv_ref, down_ref, up_ref, out_ref):
    slots, both_rows, width = recv_ref.shape
    rows = both_rows // 2
    rank = down_ref.shape[2]
    tok = recv_ref[:, :rows, :].reshape(slots * rows, width)
    grad = recv_ref[:, rows:, :].reshape(slots * rows, width)
    low = contract(tok, down_ref[0], 1, 0).astype(out_ref.dtype)
    back = contract(grad, up_ref[0], 1, 1).astype(out_ref.dtype)
    blocks, block_rows, _ = out_ref.shape
    out_ref[:, :, :rank] = low.reshape(blocks, block_rows, rank)
    out_ref[:, :, rank:] = back.reshape(blocks, block_rows, rank)


def reduce_kernel(inverse_root, place_ref, slots_ref, ranks_ref, kinds_ref, part_ref, out_ref):
    rank, _, _ = own_run(place_ref, slots_ref, ranks_ref, kinds_ref)
    extent = part_ref.shape[2] // 2
    column = lax.broadcasted_iota(jnp.int32, (1, 2 * extent), 1)
    keep = (jnp.where(column < extent, column, column - extent) < rank).astype(F32)
    factor = keep * jnp.where(column < extent, F32(inverse_root), F32(1.0))
    total = part_ref[0].astype(F32)
    for block in range(1, part_ref.shape[0]):
        total += part_ref[block].astype(F32)
    rounded = (total * factor).astype(out_ref.dtype)
    for block in range(out_ref.shape[0]):
        out_ref[block] = rounded


def scale_row(rank, extent):
    return adapter_alpha / jnp.sqrt(jnp.full((1, extent), rank, jnp.int32).astype(F32))


def home_kernel(
    inverse_root, place_ref, slots_ref, ranks_ref, kinds_ref, low_ref, down_ref, up_ref, out_ref
):
    rank, _, _ = own_run(place_ref, slots_ref, ranks_ref, kinds_ref)
    slots, both_rows, width = out_ref.shape
    rows = both_rows // 2
    extent = down_ref.shape[2]
    scale = scale_row(rank, width)
    low = low_ref[:, :, :extent].reshape(slots * rows, extent)
    back = low_ref[:, :, extent:].reshape(slots * rows, extent)
    forward = scale * contract(low, up_ref[0], 1, 0)
    backward = (scale * inverse_root) * contract(back, down_ref[0], 1, 1)
    out_ref[:, :rows, :] = forward.astype(out_ref.dtype).reshape(slots, rows, width)
    out_ref[:, rows:, :] = backward.astype(out_ref.dtype).reshape(slots, rows, width)


def grad_kernel(
    inverse_root,
    place_ref,
    slots_ref,
    ranks_ref,
    kinds_ref,
    recv_ref,
    low_ref,
    wide_ref,
    down_ref,
    up_ref,
    wide_new_ref,
    sums_ref,
):
    rank, _, _ = own_run(place_ref, slots_ref, ranks_ref, kinds_ref)
    slots, both_rows, width = recv_ref.shape
    rows = both_rows // 2
    extent = low_ref.shape[2] // 2
    tok = recv_ref[:, :rows, :].reshape(slots * rows, width)
    grad = recv_ref[:, rows:, :].reshape(slots * rows, width)
    low = low_ref[:, :, :extent].reshape(slots * rows, extent)
    back = low_ref[:, :, extent:].reshape(slots * rows, extent)
    grad_up = scale_row(rank, width) * contract(low, grad, 0, 0)
    grad_down = (scale_row(rank, extent) * inverse_root) * contract(tok, back, 0, 0)
    up_ref[...] = grad_up
    down_ref[...] = grad_down
    square_up = grad_up * grad_up
    square_down = grad_down * grad_down
    rank_row = jnp.full((1, width), rank, jnp.int32).astype(F32)
    row_new = (
        factor_decay * wide_ref[0, 0:1, :]
        + (1.0 - factor_decay) * to_row(jnp.sum(square_down, axis=1, keepdims=True)) / rank_row
    )
    col_new = (
        factor_decay * wide_ref[0, 1:2, :]
        + (1.0 - factor_decay) * jnp.sum(square_up, axis=0, keepdims=True) / rank_row
    )
    wide_new_ref[0, 0:1, :] = row_new
    wide_new_ref[0, 1:2, :] = col_new
    col_part = jnp.sum(square_down, axis=0, keepdims=True)
    row_part = to_row(jnp.sum(square_up, axis=1, keepdims=True))
    total = jnp.broadcast_to(jnp.sum(row_new, axis=1, keepdims=True), (1, extent))
    sums = jnp.concatenate(
        [col_part, row_part, total, jnp.zeros((sums_ref.shape[1] - 3, extent), F32)], axis=0
    )
    for block in range(sums_ref.shape[0]):
        sums_ref[block] = sums


def update_kernel(
    full_width,
    place_ref,
    slots_ref,
    ranks_ref,
    kinds_ref,
    grad_down_ref,
    grad_up_ref,
    wide_new_ref,
    sums_ref,
    down_ref,
    up_ref,
    down_moments_ref,
    up_moments_ref,
    wide_ref,
    rank_ref,
    new_down_ref,
    new_up_ref,
    new_down_moments_ref,
    new_up_moments_ref,
    new_wide_ref,
    new_rank_ref,
):
    rank, kind, holds = own_run(place_ref, slots_ref, ranks_ref, kinds_ref)
    extent = sums_ref.shape[2]
    is_adam = kind == 0
    held = holds == 1
    keep_row = (lax.broadcasted_iota(jnp.int32, (1, extent), 1) < rank).astype(F32)
    keep_column = (lax.broadcasted_iota(jnp.int32, (extent, 1), 0) < rank).astype(F32)
    rank_row = jnp.full((1, extent), rank, jnp.int32).astype(F32)
    sums = sums_ref[0]
    for block in range(1, sums_ref.shape[0]):
        sums = sums + sums_ref[block]
    col_new = (
        factor_decay * rank_ref[0, 0:1, :] + (1.0 - factor_decay) * sums[0:1, :] / full_width
    ) * keep_row
    row_new = (
        factor_decay * rank_ref[0, 1:2, :] + (1.0 - factor_decay) * sums[1:2, :] / full_width
    ) * keep_row
    mean_down = sums[2:3, :] / full_width
    mean_up = jnp.sum(row_new, axis=1, keepdims=True) / rank_row
    col_safe = jnp.where(keep_row > 0, col_new, 1.0)
    row_safe = to_column(jnp.where(keep_row > 0, row_new, 1.0))
    wide_row = wide_new_ref[0, 0:1, :]
    wide_col = wide_new_ref[0, 1:2, :]

    def adam(weights, moments_ref, gradient):
        first = beta_first * moments_ref[0, 0] + (1.0 - beta_first) * gradient
        second = beta_second * moments_ref[0, 1] + (1.0 - beta_second) * gradient * gradient
        return weights - adam_rate * first / (jnp.sqrt(second) + adam_eps), first, second

    def finish(weights_ref, moments_ref, gradient, step, keep, new_ref, new_moments_ref):
        weights = weights_ref[0].astype(F32)
        updated, first, second = adam(weights, moments_ref, gradient)
        factored = weights - factor_rate * step
        value = jnp.where(is_adam, updated, factored) * keep
        new_ref[0] = jnp.where(held, value, 0.0).astype(new_ref.dtype)
        new_moments_ref[0, 0] = jnp.where(
            held, jnp.where(is_adam, first * keep, moments_ref[0, 0]), 0.0
        )
        new_moments_ref[0, 1] = jnp.where(
            held, jnp.where(is_adam, second * keep, moments_ref[0, 1]), 0.0
        )

    grad_down = grad_down_ref[...]
    step_down = grad_down * jnp.sqrt(mean_down / (to_column(wide_row) * col_safe))
    finish(
        down_ref,
        down_moments_ref,
        grad_down,
        step_down,
        keep_row,
        new_down_ref,
        new_down_moments_ref,
    )
    grad_up = grad_up_ref[...]
    step_up = grad_up * jnp.sqrt(mean_up[:, :1] / (row_safe * wide_col))
    finish(
        up_ref, up_moments_ref, grad_up, step_up, keep_column, new_up_ref, new_up_moments_ref
    )
    new_wide_ref[0] = jnp.where(held, jnp.where(is_adam, wide_ref[0], wide_new_ref[0]), 0.0)
    new_rank_ref[0, 0:1, :] = jnp.where(
        held, jnp.where(is_adam, rank_ref[0, 0:1, :], col_new), 0.0
    )
    new_rank_ref[0, 1:2, :] = jnp.where(
        held, jnp.where(is_adam, rank_ref[0, 1:2, :], row_new), 0.0
    )


def output_kernel(slots_ref, own_ref, other_ref, backward_ref, home_ref, layer_ref, input_ref):
    both_rows = home_ref.shape[1]
    rows = both_rows // 2
    for run in range(slots_ref.shape[0]):
        here = slice(run * rows, (run + 1) * rows)
        terms = home_ref[slots_ref[run]].astype(F32)
        layer_ref[here, :] = (
            own_ref[here, :] + other_ref[here, :].astype(F32) + terms[:rows]
        ).astype(layer_ref.dtype)
        input_ref[here, :] = (backward_ref[here, :] + terms[rows:]).astype(input_ref.dtype)


def ring_kernel(*refs):
    count = len(refs) // 3
    for index in range(count):
        message_ref, block_ref, out_ref = refs[2 * index], refs[2 * index + 1], refs[2 * count + index]
        out_ref[...] = (message_ref[...].astype(F32) + block_ref[...].astype(F32)).astype(
            out_ref.dtype
        )


def sum_kernel(place_ref, up_ref, down_ref, block_ref, own_ref, send_ref):
    half = place_ref[1]

    def total(index):
        return (
            up_ref[index].astype(F32)
            + down_ref[index].astype(F32)
            + block_ref[index].astype(F32)
        )

    own_ref[...] = total(half)
    send_ref[...] = total(1 - half).astype(send_ref.dtype)


def local(
    tokens,
    output_gradient,
    frozen_weight,
    adapter_down,
    adapter_up,
    down_adam_moments,
    up_adam_moments,
    feature_factors,
    rank_factors,
    run_adapter_ranks,
    run_optimizers,
    run_owner_slots,
):
    slot_count = lax.axis_size("run")
    tp_count = lax.axis_size("tp")
    ring_length = tp_count // 2
    token_rows, width = tokens.shape
    full_width = frozen_weight.shape[1]
    rank_extent = adapter_down.shape[2]
    run_count = run_adapter_ranks.shape[0]
    run_rows = token_rows // run_count
    inverse_root = 1.0 / math.sqrt(full_width)
    position = lax.axis_index("run")
    tp_self = lax.axis_index("tp")
    half_self = lax.rem(tp_self, 2)
    z_self = tp_self // 2
    place = jnp.stack(
        [position, half_self]
        + [lax.rem(z_self + offset, ring_length) for offset in range(ring_length)]
    ).astype(jnp.int32)
    run_facts = (place, run_owner_slots, run_adapter_ranks, run_optimizers)
    swap_pairs = [(index, index ^ 1) for index in range(tp_count)]
    up_pairs = [(index, (index + 2) % tp_count) for index in range(tp_count)]
    down_pairs = [(index, (index - 2) % tp_count) for index in range(tp_count)]
    z_groups = [[z * 2 + half for z in range(ring_length)] for half in range(2)]

    (to_owner,) = staged_call(
        scatter_kernel,
        (shape((slot_count, 2 * run_rows, width), BF16),),
        (run_owner_slots,),
        (tokens, output_gradient),
    )
    recv = all_to_all(to_owner, "run")

    def from_every_z(values):
        return lax.all_gather(
            values[None], "tp", axis=0, tiled=True, axis_index_groups=z_groups
        )

    grad_own = from_every_z(output_gradient)
    swapped = lax.ppermute(output_gradient, "tp", swap_pairs)
    grad_other = from_every_z(swapped)

    def partial_blocks(first, stride, count, after):
        return pl.pallas_call(
            partial_kernel,
            out_shape=shape((count, 2, token_rows, width), BF16),
            grid_spec=pltpu.PrefetchScalarGridSpec(
                num_scalar_prefetch=1,
                grid=(count,),
                in_specs=[
                    pl.BlockSpec((token_rows, width), lambda i, place: (0, 0)),
                    pl.BlockSpec(
                        (width, 2 * width),
                        lambda i, place: (0, place[2 + (first + i * stride) % ring_length]),
                    ),
                    pl.BlockSpec(memory_space=pl.ANY),
                ],
                out_specs=pl.BlockSpec(
                    (1, 2, token_rows, width), lambda i, place: (i, 0, 0, 0)
                ),
            ),
            compiler_params=PARAMS,
        )(place, tokens, frozen_weight, after)

    up_steps = ring_length // 2
    down_steps = ring_length - 1 - up_steps
    first_blocks = partial_blocks(up_steps, 1, 2, to_owner)
    upward, downward = first_blocks[0], first_blocks[1]
    partial = partial_blocks(up_steps + 2, 1, ring_length - 2, first_blocks)

    def block_at(offset):
        return (partial, (offset - up_steps - 2) % ring_length)


    def hop_up(values):
        return lax.ppermute(values, "tp", up_pairs)

    def hop_down(values):
        return lax.ppermute(values, "tp", down_pairs)

    message = shape(upward.shape, BF16)

    def ring_operands(step, upward, downward):
        operands = (hop_up(upward), block_at(up_steps - step))
        if step < down_steps:
            operands += (hop_down(downward), block_at(ring_length - down_steps + step))
        return operands

    def ring_step(step, upward, downward, after):
        operands = ring_operands(step, upward, downward)
        return staged_call(
            ring_kernel, (message,) * (len(operands) // 2), (), operands, after
        )

    upward, downward = ring_step(1, upward, downward, ())
    (low_part,) = staged_call(
        low_kernel,
        (shape((tp_count, slot_count * run_rows // tp_count, 2 * rank_extent), BF16),),
        (),
        (recv, adapter_down, adapter_up),
        after=(swapped, upward, downward),
    )
    low_blocks = all_to_all(low_part, "tp")
    upward, downward = ring_step(2, upward, downward, (low_part,))
    (low_own,) = staged_call(
        functools.partial(reduce_kernel, inverse_root),
        (shape(low_blocks.shape, BF16),),
        run_facts,
        (low_blocks,),
        after=(upward, downward),
    )
    low_all = all_to_all(low_own, "tp")
    (upward,) = ring_step(3, upward, downward, (low_own,))
    (to_home,) = staged_call(
        functools.partial(home_kernel, inverse_root),
        (shape((slot_count, 2 * run_rows, width), BF16),),
        run_facts,
        (low_all, adapter_down, adapter_up),
        after=(upward,),
    )
    home = all_to_all(to_home, "run")

    base_own, base_send = staged_call(
        sum_kernel,
        (shape((token_rows, width), F32), shape((token_rows, width), BF16)),
        (place,),
        (hop_up(upward), hop_down(downward), block_at(0)),
        after=(to_home,),
    )
    base_other = lax.ppermute(base_send, "tp", swap_pairs)

    backward_total = pl.pallas_call(
        backward_kernel,
        out_shape=shape((token_rows, width), F32),
        grid_spec=pltpu.PrefetchScalarGridSpec(
            num_scalar_prefetch=1,
            grid=(ring_length,),
            in_specs=[
                pl.BlockSpec((1, token_rows, width), lambda i, place: (i, 0, 0)),
                pl.BlockSpec((1, token_rows, width), lambda i, place: (i, 0, 0)),
                pl.BlockSpec((width, 2 * width), lambda i, place: (0, i)),
            ],
            out_specs=pl.BlockSpec((token_rows, width), lambda i, place: (0, 0)),
        ),
        compiler_params=PARAMS,
    )(place, grad_own, grad_other, frozen_weight)

    grad_down, grad_up, wide_new, sums = staged_call(
        functools.partial(grad_kernel, inverse_root),
        (
            shape((width, rank_extent), F32),
            shape((rank_extent, width), F32),
            shape((1, 2, width), F32),
            shape((tp_count, 8, rank_extent), F32),
        ),
        run_facts,
        (recv, low_all, feature_factors),
        after=(home, backward_total, base_other),
    )
    all_sums = all_to_all(sums, "tp")
    layer_output, input_gradient = staged_call(
        output_kernel,
        (shape((token_rows, width), BF16),) * 2,
        (run_owner_slots,),
        (base_own, base_other, backward_total, home),
        after=(sums,),
    )
    updated = staged_call(
        functools.partial(update_kernel, full_width),
        (
            shape(adapter_down.shape, BF16),
            shape(adapter_up.shape, BF16),
            shape(down_adam_moments.shape, F32),
            shape(up_adam_moments.shape, F32),
            shape(feature_factors.shape, F32),
            shape(rank_factors.shape, F32),
        ),
        run_facts,
        (
            grad_down,
            grad_up,
            wide_new,
            all_sums,
            adapter_down,
            adapter_up,
            down_adam_moments,
            up_adam_moments,
            feature_factors,
            rank_factors,
        ),
        after=(layer_output,),
    )
    return (layer_output, input_gradient) + tuple(updated)


def solution(mesh):
    placed = (
        P("run", "tp"),
        P("run", "tp"),
        P("tp", None),
        P("run", "tp", None),
        P("run", None, "tp"),
        P("run", None, "tp", None),
        P("run", None, None, "tp"),
        P("run", None, "tp"),
        P("run", None, None),
        P(),
        P(),
        P(),
    )
    return jax.shard_map(
        local,
        mesh=mesh,
        in_specs=placed,
        out_specs=(
            P("run", "tp"),
            P("run", "tp"),
            P("run", "tp", None),
            P("run", None, "tp"),
            P("run", None, "tp", None),
            P("run", None, None, "tp"),
            P("run", None, "tp"),
            P("run", None, None),
        ),
        check_vma=False,
    )
```
